32 devices in a mesh: trial: 2 (over x), wide: 8 (over z, y), narrow: 2 (over core).
Axes of the slice: x: 2, y: 2, z: 4, core: 2. Of those that a mesh axis runs over, the one named last changes fastest.
Arguments:
- points: float32 [32, 32768], P(None, ('trial', 'wide', 'narrow')), parts along dimension 1, may hold values from -6 to 6
- probes: bfloat16 [17, 32768], P(None, ('trial', 'wide', 'narrow')), parts along dimension 1, may hold values from -6 to 6
- lengthscale: float32 [64], P('trial'), parts along dimension 0, may hold values from 1.5 to 4
- noise: float32 [2], P('trial'), parts along dimension 0, may hold values from 0.3 to 1.5
Outputs:
- product: float32 [17, 32768], P(None, ('trial', 'wide', 'narrow')), parts along dimension 1
The draws below stay inside these ranges and needn't reach their ends.
There are 2 independent parts, one for each index of `trial`. The reference program is written for one: setup_inputs(seed, part) draws one part's arguments, and reference() takes and returns one part's arrays. A program takes and returns all parts, laid end to end along the dimension named above; each array names one. Nothing has to cross between parts.
All inputs are finite; a program needn't handle non-finite values.
Results may differ from the reference program's by a relative error of at most 0.0046.
Values may be sent and summed in bfloat16 or wider, within the bound.
A program may use at most 64 MiB of HBM per device.

```python
import math
import jax
import jax.numpy as jnp
from jax import lax

F = 32
R = 17
PTS_DEV = 1024
NPTS = 16384


def shard_levels(own_key, extent, split, low, high):
    factor_of = 1.0
    for dim, shards_of in split:
        draws = jax.random.uniform(jax.random.fold_in(jax.random.fold_in(own_key, 6), dim), (shards_of,), jnp.float32, low / len(split), high / len(split))
        factor_of = factor_of * jnp.repeat(jnp.exp(draws), extent[dim] // shards_of).reshape((-1,) + (1,) * (len(extent) - 1 - dim))
    return factor_of


def bell_draw(key, dims, scale, reach, shards=(), kind=jnp.bfloat16):
    array = scale * jax.random.normal(key, dims, jnp.float32)
    if shards:
        array = array * shard_levels(key, dims, shards, -0.22, 0.18)
    return jnp.clip(array, -reach, reach).astype(kind)


def setup_inputs(seed: int = 0, part: int = 0) -> dict:
    keys = jax.random.split(jax.random.key(seed), 5)
    part_splits = jax.random.split(jax.random.fold_in(keys[4], part), 5)
    return {
        "points": bell_draw(part_splits[0], (F, NPTS), 1.0, 6.0, ((1, 16),), jnp.float32),
        "probes": bell_draw(part_splits[1], (R, NPTS), 1.0, 6.0, ((1, 16),)),
        "lengthscale": jnp.clip(jnp.exp(jax.random.uniform(part_splits[2], (F,), jnp.float32, math.log(1.5), math.log(4.0))), 1.5, 4.0),
        "noise": jnp.clip(jnp.exp(jax.random.uniform(part_splits[3], (1,), jnp.float32, math.log(0.3), math.log(1.5))), 0.3, 1.5),
    }


def reference(points, probes, lengthscale, noise):
    scaled = (points / lengthscale[:, None]).astype(jnp.bfloat16)
    wide_f = scaled.astype(jnp.float32)
    norms = jnp.sum(wide_f * wide_f, axis=0)
    block = 2 * PTS_DEV
    count = NPTS // block

    def one_block(index):
        start = (index * block).astype(jnp.int32)
        rows_x = lax.dynamic_slice_in_dim(scaled, start, block, 1)
        rows_n = lax.dynamic_slice_in_dim(norms, start, block, 0)
        cross = lax.dot_general(rows_x, scaled, (((0,), (0,)), ((), ())), preferred_element_type=jnp.float32)
        kernel = jnp.exp(-0.5 * (rows_n[:, None] + norms[None, :] - 2.0 * cross)).astype(jnp.bfloat16)
        return lax.dot_general(probes, kernel, (((1,), (1,)), ((), ())), preferred_element_type=jnp.float32)

    parts = lax.map(one_block, jnp.arange(count, dtype=jnp.int32))
    summed = jnp.transpose(parts, (1, 0, 2)).reshape(R, NPTS)
    return summed + noise[0] * probes.astype(jnp.float32)
```

```python
import functools
import math

import jax
import jax.numpy as jnp
from jax import lax
from jax.experimental import pallas as pl
from jax.experimental.pallas import tpu as pltpu
from jax.sharding import PartitionSpec as P

LOG2E = math.log2(math.e)
NT = (((1,), (1,)), ((), ()))
TN = (((0,), (0,)), ((), ()))


def three_parts(value):
    high = value.astype(jnp.bfloat16).astype(jnp.float32)
    rest = value - high
    middle = rest.astype(jnp.bfloat16).astype(jnp.float32)
    return high, middle, rest - middle


def flipped(index, mask, bits):
    for b in range(bits):
        p = 2**b
        index = index + ((mask // p) % 2) * p * (1 - 2 * ((index // p) % 2))
    return index


def kernel(wide, points_ref, probes_ref, length_ref, out_ref, held, own, visit, pad, acc,
           send_sem, recv_sem):
    t, w, c = lax.axis_index("trial"), lax.axis_index("wide"), lax.axis_index("narrow")
    feats, pts = points_ref.shape
    cols = probes_ref.shape[0]
    lines = wide // 2
    bits = lines.bit_length() - 1
    z, y = w // 2, w % 2

    def place(j, side):
        return flipped(z, j, bits) * 2 + y + side * (1 - 2 * y)

    across = place(0, 1)
    barrier = pltpu.get_barrier_semaphore()
    peers = [(t, w, 1 - c), (t, across, c)] + [(t, place(j, 0), c) for j in range(1, lines)]
    for peer in peers:
        pl.semaphore_signal(barrier, inc=1, device_id=peer, device_id_type=pl.DeviceIdType.MESH)

    mine = held.at[w * 2 + c]
    scaled = (points_ref[...] / length_ref[...]).astype(jnp.bfloat16)
    wide_f = scaled.astype(jnp.float32)
    norm = jnp.sum(wide_f * wide_f, axis=0, keepdims=True)
    n_parts = three_parts((-0.5 * LOG2E) * norm)
    pad[...] = jnp.zeros_like(pad)
    pad[:cols] = probes_ref[...].astype(jnp.float32)
    row = lax.broadcasted_iota(jnp.int32, (32, pts), 0)
    tail = pad[...]
    mirror = jnp.zeros((32, pts), jnp.float32)
    for k, part in enumerate(n_parts):
        tail = jnp.where(row == cols + k, part, tail)
        tail = jnp.where(row == cols + 3 + k, 1.0, tail)
        mirror = jnp.where(row == cols + k, 1.0, mirror)
        mirror = jnp.where(row == cols + 3 + k, part, mirror)
    mine[:feats] = scaled
    mine[feats:] = tail.astype(jnp.bfloat16)

    pl.semaphore_wait(barrier, len(peers))

    def copy(slot, kind, device):
        return pltpu.make_async_remote_copy(
            src_ref=held.at[slot], dst_ref=held.at[slot],
            send_sem=send_sem.at[kind], recv_sem=recv_sem.at[slot],
            device_id=device, device_id_type=pl.DeviceIdType.MESH)

    def arrived(slot):
        copy(slot, 0, (t, w, c)).wait_recv()

    def to_sibling(o):
        return copy(place(o // 2, o % 2) * 2 + c, o, (t, w, 1 - c))

    def to_across(j):
        return copy(place(j, 0) * 2 + c, wide + j, (t, across, c))

    def along(j):
        return copy(w * 2 + c, wide + lines + j, (t, place(j, 0), c))

    to_across(0).start()
    to_sibling(0).start()
    for j in range(1, lines):
        along(j).start()

    for k, part in enumerate(three_parts(wide_f * LOG2E)):
        own[feats * k:feats * (k + 1)] = part.astype(jnp.bfloat16)
    own[3 * feats:] = mirror.astype(jnp.bfloat16)
    acc[...] = jnp.zeros_like(acc)

    def step(s, _):
        o, half = s // 2, s % 2
        slot = place(o // 2, o % 2) * 2 + c + half * (1 - 2 * c)

        @pl.when((half == 0) & (o % 2 == 1))
        def _():
            arrived(slot)
            to_sibling(o).start()

        @pl.when(half == 1)
        def _():
            arrived(slot)

            @pl.when((o % 2 == 1) & (o + 1 < wide))
            def _():
                j = (o + 1) // 2
                arrived(place(j, 0) * 2 + c)
                to_across(j).start()
                to_sibling(o + 1).start()

        block = held.at[slot]
        for k in range(3):
            visit[feats * k:feats * (k + 1)] = block[:feats]
        visit[3 * feats:] = block[feats:]
        cross = lax.dot_general(visit[...], own[...], TN, preferred_element_type=jnp.float32)
        tile = jnp.exp2(cross).astype(jnp.bfloat16)
        acc[...] += jnp.dot(block[feats:], tile, preferred_element_type=jnp.float32)
        return 0

    lax.fori_loop(0, 2 * wide, step, 0)
    out_ref[...] = acc[:cols]

    for o in range(wide):
        to_sibling(o).wait_send()
    for j in range(lines):
        to_across(j).wait_send()
    for j in range(1, lines):
        along(j).wait_send()


def solution(mesh):
    wide = mesh.shape["wide"]

    def body(points, probes, lengthscale, noise):
        feats, pts = points.shape
        cols = probes.shape[0]
        rows = feats + 32
        summed = pl.pallas_call(
            functools.partial(kernel, wide),
            out_shape=jax.ShapeDtypeStruct((cols, pts), jnp.float32),
            in_specs=[pl.BlockSpec(memory_space=pltpu.VMEM)] * 3,
            out_specs=pl.BlockSpec(memory_space=pltpu.VMEM),
            scratch_shapes=[
                pltpu.VMEM((2 * wide, rows, pts), jnp.bfloat16),
                pltpu.VMEM((3 * feats + 32, pts), jnp.bfloat16),
                pltpu.VMEM((3 * feats + 32, pts), jnp.bfloat16),
                pltpu.VMEM((32, pts), jnp.float32),
                pltpu.VMEM((32, pts), jnp.float32),
                pltpu.SemaphoreType.DMA((2 * wide,)),
                pltpu.SemaphoreType.DMA((2 * wide,)),
            ],
            compiler_params=pltpu.CompilerParams(
                collective_id=0, has_side_effects=True, vmem_limit_bytes=40 * 2**20),
        )(points, probes, lengthscale[:, None])
        return summed + noise[0] * probes.astype(jnp.float32)

    placed = (
        P(None, ("trial", "wide", "narrow")),
        P(None, ("trial", "wide", "narrow")),
        P("trial"),
        P("trial"),
    )
    return jax.shard_map(
        body, mesh=mesh, in_specs=placed,
        out_specs=P(None, ("trial", "wide", "narrow")), check_vma=False)
```

```python
import functools
import math

import jax
import jax.numpy as jnp
from jax import lax
from jax.experimental import pallas as pl
from jax.experimental.pallas import tpu as pltpu
from jax.sharding import PartitionSpec as P

LOG2E = math.log2(math.e)
NT = (((1,), (1,)), ((), ()))
TN = (((0,), (0,)), ((), ()))


def three_parts(value):
    high = value.astype(jnp.bfloat16).astype(jnp.float32)
    rest = value - high
    middle = rest.astype(jnp.bfloat16).astype(jnp.float32)
    return high, middle, rest - middle


def flipped(index, mask, bits):
    for b in range(bits):
        p = 2**b
        index = index + ((mask // p) % 2) * p * (1 - 2 * ((index // p) % 2))
    return index


def kernel(wide, points_hbm, probes_hbm, length_hbm, out_ref, held, own, visit, pad, acc,
           points_ref, probes_ref, length_ref, load_sem, send_sem, recv_sem):
    loads = [pltpu.make_async_copy(a, b, load_sem.at[i]) for i, (a, b) in enumerate(
        [(points_hbm, points_ref), (probes_hbm, probes_ref), (length_hbm, length_ref)])]
    for load in loads:
        load.start()
    t, w, c = lax.axis_index("trial"), lax.axis_index("wide"), lax.axis_index("narrow")
    feats, pts = points_ref.shape
    cols = probes_ref.shape[0]
    lines = wide // 2
    bits = lines.bit_length() - 1
    z, y = w // 2, w % 2

    def place(j, side):
        return flipped(z, j, bits) * 2 + y + side * (1 - 2 * y)

    across = place(0, 1)
    barrier = pltpu.get_barrier_semaphore()
    peers = [(t, w, 1 - c), (t, across, c)] + [(t, place(j, 0), c) for j in range(1, lines)]
    for peer in peers:
        pl.semaphore_signal(barrier, inc=1, device_id=peer, device_id_type=pl.DeviceIdType.MESH)

    for load in loads:
        load.wait()
    mine = held.at[w * 2 + c]
    scaled = (points_ref[...] / length_ref[...]).astype(jnp.bfloat16)
    wide_f = scaled.astype(jnp.float32)
    norm = jnp.sum(wide_f * wide_f, axis=0, keepdims=True)
    n_parts = three_parts((-0.5 * LOG2E) * norm)
    pad[...] = jnp.zeros_like(pad)
    pad[:cols] = probes_ref[...].astype(jnp.float32)
    row = lax.broadcasted_iota(jnp.int32, (32, pts), 0)
    tail = pad[...]
    mirror = jnp.zeros((32, pts), jnp.float32)
    for k, part in enumerate(n_parts):
        tail = jnp.where(row == cols + k, part, tail)
        tail = jnp.where(row == cols + 3 + k, 1.0, tail)
        mirror = jnp.where(row == cols + k, 1.0, mirror)
        mirror = jnp.where(row == cols + 3 + k, part, mirror)
    mine[:feats] = scaled
    mine[feats:] = tail.astype(jnp.bfloat16)

    pl.semaphore_wait(barrier, len(peers))

    def copy(slot, kind, device):
        return pltpu.make_async_remote_copy(
            src_ref=held.at[slot], dst_ref=held.at[slot],
            send_sem=send_sem.at[kind], recv_sem=recv_sem.at[slot],
            device_id=device, device_id_type=pl.DeviceIdType.MESH)

    def arrived(slot):
        copy(slot, 0, (t, w, c)).wait_recv()

    def item(k):
        odd, later, last = k % 2, (k + wide - 1) // wide, (k + 1) // wide
        j = odd * ((k + 1) // 2 - last) + (1 - odd) * (k // 2 - later)
        return j, odd * last + (1 - odd) * later

    def slot_of(k):
        return place(*item(k)) * 2 + c

    def to_sibling(k):
        return copy(slot_of(k), k, (t, w, 1 - c))

    def to_across(j):
        return copy(place(j, 0) * 2 + c, wide + j, (t, across, c))

    def along(j):
        return copy(w * 2 + c, wide + lines + j, (t, place(j, 0), c))

    to_across(0).start()
    for j in range(1, lines):
        along(j).start()
    to_sibling(0).start()

    for k, part in enumerate(three_parts(wide_f * LOG2E)):
        own[feats * k:feats * (k + 1)] = part.astype(jnp.bfloat16)
    own[3 * feats:] = mirror.astype(jnp.bfloat16)
    acc[...] = jnp.zeros_like(acc)

    def forward(k):
        j, side = item(k)
        arrived(slot_of(k))

        @pl.when(side == 0)
        def _():
            to_across(j).start()

        to_sibling(k).start()

    def step(s, _):
        o, half = s // 2, s % 2
        slot = slot_of(o) + half * (1 - 2 * c)

        @pl.when(s == 2)
        def _():
            forward(1)
            forward(2)

        @pl.when(half == 1)
        def _():
            arrived(slot)

            @pl.when((o >= 2) & (o + 1 < wide))
            def _():
                forward(o + 1)

        block = held.at[slot]
        for k in range(3):
            visit[feats * k:feats * (k + 1)] = block[:feats]
        visit[3 * feats:] = block[feats:]
        cross = lax.dot_general(visit[...], own[...], TN, preferred_element_type=jnp.float32)
        tile = jnp.exp2(cross).astype(jnp.bfloat16)
        acc[...] += jnp.dot(block[feats:], tile, preferred_element_type=jnp.float32)
        return 0

    lax.fori_loop(0, 2 * wide, step, 0)
    out_ref[...] = acc[:cols]

    for o in range(wide):
        to_sibling(o).wait_send()
    for j in range(lines):
        to_across(j).wait_send()
    for j in range(1, lines):
        along(j).wait_send()


def solution(mesh):
    wide = mesh.shape["wide"]

    def body(points, probes, lengthscale, noise):
        feats, pts = points.shape
        cols = probes.shape[0]
        rows = feats + 32
        summed = pl.pallas_call(
            functools.partial(kernel, wide),
            out_shape=jax.ShapeDtypeStruct((cols, pts), jnp.float32),
            in_specs=[pl.BlockSpec(memory_space=pltpu.HBM)] * 3,
            out_specs=pl.BlockSpec(memory_space=pltpu.VMEM),
            scratch_shapes=[
                pltpu.VMEM((2 * wide, rows, pts), jnp.bfloat16),
                pltpu.VMEM((3 * feats + 32, pts), jnp.bfloat16),
                pltpu.VMEM((3 * feats + 32, pts), jnp.bfloat16),
                pltpu.VMEM((32, pts), jnp.float32),
                pltpu.VMEM((32, pts), jnp.float32),
                pltpu.VMEM((feats, pts), points.dtype),
                pltpu.VMEM((cols, pts), probes.dtype),
                pltpu.VMEM((feats, 1), lengthscale.dtype),
                pltpu.SemaphoreType.DMA((3,)),
                pltpu.SemaphoreType.DMA((2 * wide,)),
                pltpu.SemaphoreType.DMA((2 * wide,)),
            ],
            compiler_params=pltpu.CompilerParams(
                collective_id=0, has_side_effects=True, vmem_limit_bytes=40 * 2**20),
        )(points, probes, lengthscale[:, None])
        return summed + noise[0] * probes.astype(jnp.float32)

    placed = (
        P(None, ("trial", "wide", "narrow")),
        P(None, ("trial", "wide", "narrow")),
        P("trial"),
        P("trial"),
    )
    return jax.shard_map(
        body, mesh=mesh, in_specs=placed,
        out_specs=P(None, ("trial", "wide", "narrow")), check_vma=False)
```

```python
import functools
import math

import jax
import jax.numpy as jnp
from jax import lax
from jax.experimental import pallas as pl
from jax.experimental.pallas import tpu as pltpu
from jax.sharding import PartitionSpec as P

LOG2E = math.log2(math.e)
NT = (((1,), (1,)), ((), ()))
TN = (((0,), (0,)), ((), ()))


def three_parts(value):
    high = value.astype(jnp.bfloat16).astype(jnp.float32)
    rest = value - high
    middle = rest.astype(jnp.bfloat16).astype(jnp.float32)
    return high, middle, rest - middle


def kernel(wide, points_hbm, probes_hbm, length_hbm, out_ref, held, own, visit, pad, acc,
           points_ref, probes_ref, length_ref, load_sem, sib_sem, side_sem, up_sem, down_sem,
           recv_sem):
    loads = [pltpu.make_async_copy(a, b, load_sem.at[i]) for i, (a, b) in enumerate(
        [(points_hbm, points_ref), (probes_hbm, probes_ref), (length_hbm, length_ref)])]
    for load in loads:
        load.start()
    t, w, c = lax.axis_index("trial"), lax.axis_index("wide"), lax.axis_index("narrow")
    feats, pts = points_ref.shape
    cols = probes_ref.shape[0]
    lines = wide // 2
    z, y = w // 2, w % 2
    upper = z * 2 // lines
    paired = z * (1 - upper) + (lines - 1 - z) * upper
    far = 4 * lines

    def at_rank(r):
        lone = (r + far - 2 * paired - 1) // far
        step = (1 - lone) * ((r + 1) // 2) * (2 * ((r + 1) % 2) - 1) + lone * (r - paired) * (1 - 2 * upper)
        return z + step

    def place(line, side):
        return line * 2 + y + side * (1 - 2 * y)

    across = place(z, 1)
    barrier = pltpu.get_barrier_semaphore()
    for peer in [(t, w, 1 - c), (t, across, c)]:
        pl.semaphore_signal(barrier, inc=1, device_id=peer, device_id_type=pl.DeviceIdType.MESH)

    @pl.when(z > 0)
    def _():
        pl.semaphore_signal(barrier, inc=1, device_id=(t, w - 2, c), device_id_type=pl.DeviceIdType.MESH)

    @pl.when(z < lines - 1)
    def _():
        pl.semaphore_signal(barrier, inc=1, device_id=(t, w + 2, c), device_id_type=pl.DeviceIdType.MESH)

    for load in loads:
        load.wait()
    mine = held.at[w * 2 + c]
    scaled = (points_ref[...] / length_ref[...]).astype(jnp.bfloat16)
    wide_f = scaled.astype(jnp.float32)
    norm = jnp.sum(wide_f * wide_f, axis=0, keepdims=True)
    n_parts = three_parts((-0.5 * LOG2E) * norm)
    pad[...] = jnp.zeros_like(pad)
    pad[:cols] = probes_ref[...].astype(jnp.float32)
    row = lax.broadcasted_iota(jnp.int32, (32, pts), 0)
    tail = pad[...]
    mirror = jnp.zeros((32, pts), jnp.float32)
    for k, part in enumerate(n_parts):
        tail = jnp.where(row == cols + k, part, tail)
        tail = jnp.where(row == cols + 3 + k, 1.0, tail)
        mirror = jnp.where(row == cols + k, 1.0, mirror)
        mirror = jnp.where(row == cols + 3 + k, part, mirror)
    mine[:feats] = scaled
    mine[feats:] = tail.astype(jnp.bfloat16)

    ends = (z + lines - 1) // lines + (2 * lines - 2 - z) // lines
    pl.semaphore_wait(barrier, 2 + ends)

    def copy(where, half, sems, device):
        rows = pl.ds(half * feats, feats if half == 0 else 32)
        return pltpu.make_async_remote_copy(
            src_ref=held.at[where * 2 + c, rows], dst_ref=held.at[where * 2 + c, rows],
            send_sem=sems.at[where * 2 + half], recv_sem=recv_sem.at[(where * 2 + c) * 2 + half],
            device_id=device, device_id_type=pl.DeviceIdType.MESH)

    def arrived(slot, half):
        rows = pl.ds(half * feats, feats if half == 0 else 32)
        pltpu.make_async_remote_copy(
            src_ref=held.at[slot, rows], dst_ref=held.at[slot, rows],
            send_sem=sib_sem.at[half], recv_sem=recv_sem.at[slot * 2 + half],
            device_id=(t, w, 1 - c), device_id_type=pl.DeviceIdType.MESH).wait_recv()

    def to_sibling(where, half):
        return copy(where, half, sib_sem, (t, w, 1 - c))

    def to_across(where, half):
        return copy(where, half, side_sem, (t, across, c))

    def upward(where, half):
        return copy(where, half, up_sem, (t, w + 2, c))

    def downward(where, half):
        return copy(where, half, down_sem, (t, w - 2, c))

    for half in range(2):
        to_across(w, half).start()

        @pl.when(z < lines - 1)
        def _():
            upward(w, half).start()

        @pl.when(z > 0)
        def _():
            downward(w, half).start()

        to_sibling(w, half).start()

    for k, part in enumerate(three_parts(wide_f * LOG2E)):
        own[feats * k:feats * (k + 1)] = part.astype(jnp.bfloat16)
    own[3 * feats:] = mirror.astype(jnp.bfloat16)
    acc[...] = jnp.zeros_like(acc)

    def from_line(d, half):
        @pl.when(z - d >= 0)
        def _():
            below = w - 2 * d
            arrived(below * 2 + c, half)

            @pl.when(z < lines - 1)
            def _():
                upward(below, half).start()

            to_across(below, half).start()
            to_sibling(below, half).start()

        @pl.when(z + d < lines)
        def _():
            above = w + 2 * d
            arrived(above * 2 + c, half)

            @pl.when(z > 0)
            def _():
                downward(above, half).start()

            to_across(above, half).start()
            to_sibling(above, half).start()

    def where_of(k):
        odd, later, last = k % 2, (k + wide - 1) // wide, (k + 1) // wide
        rank = odd * ((k + 1) // 2 - last) + (1 - odd) * (k // 2 - later)
        return place(at_rank(rank), odd * last + (1 - odd) * later)

    def step(s, _):
        o, half = s // 2, s % 2
        slot = where_of(o) * 2 + c + half * (1 - 2 * c)

        @pl.when(s == 2)
        def _():
            from_line(1, 0)
            from_line(1, 1)

        @pl.when((s % 3 == 1) & (s >= 4))
        def _():
            from_line((s + 2) // 3, 0)

        @pl.when((s % 3 == 2) & (s >= 5))
        def _():
            from_line((s + 1) // 3, 1)

        @pl.when(half == 1)
        def _():
            arrived(slot, 0)
            arrived(slot, 1)
            k = o + 1

            @pl.when(((k % 2 == 0) & (k < wide)) | (k == wide - 1))
            def _():
                there = where_of(k)
                for part in range(2):
                    arrived(there * 2 + c, part)
                    to_sibling(there, part).start()

        block = held.at[slot]
        for k in range(3):
            visit[feats * k:feats * (k + 1)] = block[:feats]
        visit[3 * feats:] = block[feats:]
        cross = lax.dot_general(visit[...], own[...], TN, preferred_element_type=jnp.float32)
        tile = jnp.exp2(cross).astype(jnp.bfloat16)
        acc[...] += jnp.dot(block[feats:], tile, preferred_element_type=jnp.float32)
        return 0

    lax.fori_loop(0, 2 * wide, step, 0)
    out_ref[...] = acc[:cols]

    for half in range(2):
        for where in range(wide):
            to_sibling(where, half).wait_send()
        for line in range(lines):
            to_across(place(line, 0), half).wait_send()

            @pl.when((line <= z) & (z < lines - 1))
            def _():
                upward(place(line, 0), half).wait_send()

            @pl.when((line >= z) & (z > 0))
            def _():
                downward(place(line, 0), half).wait_send()


def solution(mesh):
    wide = mesh.shape["wide"]

    def body(points, probes, lengthscale, noise):
        feats, pts = points.shape
        cols = probes.shape[0]
        rows = feats + 32
        summed = pl.pallas_call(
            functools.partial(kernel, wide),
            out_shape=jax.ShapeDtypeStruct((cols, pts), jnp.float32),
            in_specs=[pl.BlockSpec(memory_space=pltpu.HBM)] * 3,
            out_specs=pl.BlockSpec(memory_space=pltpu.VMEM),
            scratch_shapes=[
                pltpu.VMEM((2 * wide, rows, pts), jnp.bfloat16),
                pltpu.VMEM((3 * feats + 32, pts), jnp.bfloat16),
                pltpu.VMEM((3 * feats + 32, pts), jnp.bfloat16),
                pltpu.VMEM((32, pts), jnp.float32),
                pltpu.VMEM((32, pts), jnp.float32),
                pltpu.VMEM((feats, pts), points.dtype),
                pltpu.VMEM((cols, pts), probes.dtype),
                pltpu.VMEM((feats, 1), lengthscale.dtype),
                pltpu.SemaphoreType.DMA((3,)),
                pltpu.SemaphoreType.DMA((2 * wide,)),
                pltpu.SemaphoreType.DMA((2 * wide,)),
                pltpu.SemaphoreType.DMA((2 * wide,)),
                pltpu.SemaphoreType.DMA((2 * wide,)),
                pltpu.SemaphoreType.DMA((4 * wide,)),
            ],
            compiler_params=pltpu.CompilerParams(
                collective_id=0, has_side_effects=True, vmem_limit_bytes=64 * 2**20 - 2**17),
        )(points, probes, lengthscale[:, None])
        return summed + noise[0] * probes.astype(jnp.float32)

    placed = (
        P(None, ("trial", "wide", "narrow")),
        P(None, ("trial", "wide", "narrow")),
        P("trial"),
        P("trial"),
    )
    return jax.shard_map(
        body, mesh=mesh, in_specs=placed,
        out_specs=P(None, ("trial", "wide", "narrow")), check_vma=False)
```

```python
import functools
import math

import jax
import jax.numpy as jnp
from jax import lax
from jax.experimental import pallas as pl
from jax.experimental.pallas import tpu as pltpu
from jax.sharding import PartitionSpec as P

LOG2E = math.log2(math.e)
NT = (((1,), (1,)), ((), ()))
TN = (((0,), (0,)), ((), ()))


def three_parts(value):
    high = value.astype(jnp.bfloat16).astype(jnp.float32)
    rest = value - high
    middle = rest.astype(jnp.bfloat16).astype(jnp.float32)
    return high, middle, rest - middle


def kernel(wide, points_hbm, probes_hbm, length_hbm, noise_hbm, out_ref, held, own, visit, pad, acc,
           points_ref, probes_ref, length_ref, noise_ref, load_sem, sib_sem, side_sem, up_sem, down_sem,
           recv_sem):
    loads = [pltpu.make_async_copy(a, b, load_sem.at[i]) for i, (a, b) in enumerate(
        [(points_hbm, points_ref), (probes_hbm, probes_ref), (length_hbm, length_ref),
         (noise_hbm, noise_ref)])]
    for load in loads:
        load.start()
    t, w, c = lax.axis_index("trial"), lax.axis_index("wide"), lax.axis_index("narrow")
    feats, pts = points_ref.shape
    cols = probes_ref.shape[0]
    lines = wide // 2
    z, y = w // 2, w % 2
    upper = z * 2 // lines
    paired = z * (1 - upper) + (lines - 1 - z) * upper
    far = 4 * lines

    def at_rank(r):
        lone = (r + far - 2 * paired - 1) // far
        step = (1 - lone) * ((r + 1) // 2) * (2 * ((r + 1) % 2) - 1) + lone * (r - paired) * (1 - 2 * upper)
        return z + step

    def place(line, side):
        return line * 2 + y + side * (1 - 2 * y)

    across = place(z, 1)
    barrier = pltpu.get_barrier_semaphore()
    for peer in [(t, w, 1 - c), (t, across, c)]:
        pl.semaphore_signal(barrier, inc=1, device_id=peer, device_id_type=pl.DeviceIdType.MESH)

    @pl.when(z > 0)
    def _():
        pl.semaphore_signal(barrier, inc=1, device_id=(t, w - 2, c), device_id_type=pl.DeviceIdType.MESH)

    @pl.when(z < lines - 1)
    def _():
        pl.semaphore_signal(barrier, inc=1, device_id=(t, w + 2, c), device_id_type=pl.DeviceIdType.MESH)

    for load in loads:
        load.wait()
    mine = held.at[w * 2 + c]
    square = (feats, feats)
    diagonal = lax.broadcasted_iota(jnp.int32, square, 0) == lax.broadcasted_iota(jnp.int32, square, 1)
    length = jnp.sum(jnp.where(diagonal, length_ref[...], 0.0), axis=1, keepdims=True)
    scaled = (points_ref[...] / length).astype(jnp.bfloat16)
    wide_f = scaled.astype(jnp.float32)
    norm = jnp.sum(wide_f * wide_f, axis=0, keepdims=True)
    n_parts = three_parts((-0.5 * LOG2E) * norm)
    pad[...] = jnp.zeros_like(pad)
    pad[:cols] = probes_ref[...].astype(jnp.float32)
    row = lax.broadcasted_iota(jnp.int32, (32, pts), 0)
    tail = pad[...]
    mirror = jnp.zeros((32, pts), jnp.float32)
    for k, part in enumerate(n_parts):
        tail = jnp.where(row == cols + k, part, tail)
        tail = jnp.where(row == cols + 3 + k, 1.0, tail)
        mirror = jnp.where(row == cols + k, 1.0, mirror)
        mirror = jnp.where(row == cols + 3 + k, part, mirror)
    mine[:feats] = scaled
    mine[feats:] = tail.astype(jnp.bfloat16)

    ends = (z + lines - 1) // lines + (2 * lines - 2 - z) // lines
    pl.semaphore_wait(barrier, 2 + ends)

    def copy(where, half, sems, device):
        rows = pl.ds(half * feats, feats if half == 0 else 32)
        return pltpu.make_async_remote_copy(
            src_ref=held.at[where * 2 + c, rows], dst_ref=held.at[where * 2 + c, rows],
            send_sem=sems.at[where * 2 + half], recv_sem=recv_sem.at[(where * 2 + c) * 2 + half],
            device_id=device, device_id_type=pl.DeviceIdType.MESH)

    def arrived(slot, half):
        rows = pl.ds(half * feats, feats if half == 0 else 32)
        pltpu.make_async_remote_copy(
            src_ref=held.at[slot, rows], dst_ref=held.at[slot, rows],
            send_sem=sib_sem.at[half], recv_sem=recv_sem.at[slot * 2 + half],
            device_id=(t, w, 1 - c), device_id_type=pl.DeviceIdType.MESH).wait_recv()

    def to_sibling(where, half):
        return copy(where, half, sib_sem, (t, w, 1 - c))

    def to_across(where, half):
        return copy(where, half, side_sem, (t, across, c))

    def upward(where, half):
        return copy(where, half, up_sem, (t, w + 2, c))

    def downward(where, half):
        return copy(where, half, down_sem, (t, w - 2, c))

    for half in range(2):
        to_across(w, half).start()

        @pl.when(z < lines - 1)
        def _():
            upward(w, half).start()

        @pl.when(z > 0)
        def _():
            downward(w, half).start()

        to_sibling(w, half).start()

    for k, part in enumerate(three_parts(wide_f * LOG2E)):
        own[feats * k:feats * (k + 1)] = part.astype(jnp.bfloat16)
    own[3 * feats:] = mirror.astype(jnp.bfloat16)
    acc[...] = jnp.zeros_like(acc)

    def from_line(d, half):
        @pl.when(z - d >= 0)
        def _():
            below = w - 2 * d
            arrived(below * 2 + c, half)

            @pl.when(z < lines - 1)
            def _():
                upward(below, half).start()

            to_across(below, half).start()
            to_sibling(below, half).start()

        @pl.when(z + d < lines)
        def _():
            above = w + 2 * d
            arrived(above * 2 + c, half)

            @pl.when(z > 0)
            def _():
                downward(above, half).start()

            to_across(above, half).start()
            to_sibling(above, half).start()

    def where_of(k):
        odd, later, last = k % 2, (k + wide - 1) // wide, (k + 1) // wide
        rank = odd * ((k + 1) // 2 - last) + (1 - odd) * (k // 2 - later)
        return place(at_rank(rank), odd * last + (1 - odd) * later)

    def step(s, _):
        o, half = s // 2, s % 2
        slot = where_of(o) * 2 + c + half * (1 - 2 * c)

        @pl.when(s == 2)
        def _():
            from_line(1, 0)
            from_line(1, 1)

        @pl.when((s % 3 == 1) & (s >= 4))
        def _():
            from_line((s + 2) // 3, 0)

        @pl.when((s % 3 == 2) & (s >= 5))
        def _():
            from_line((s + 1) // 3, 1)

        @pl.when(half == 1)
        def _():
            arrived(slot, 0)
            arrived(slot, 1)
            k = o + 1

            @pl.when(((k % 2 == 0) & (k < wide)) | (k == wide - 1))
            def _():
                there = where_of(k)
                for part in range(2):
                    arrived(there * 2 + c, part)
                    to_sibling(there, part).start()

        block = held.at[slot]
        for k in range(3):
            visit[feats * k:feats * (k + 1)] = block[:feats]
        visit[3 * feats:] = block[feats:]
        cross = lax.dot_general(visit[...], own[...], TN, preferred_element_type=jnp.float32)
        tile = jnp.exp2(cross).astype(jnp.bfloat16)
        acc[...] += jnp.dot(block[feats:], tile, preferred_element_type=jnp.float32)
        return 0

    lax.fori_loop(0, 2 * wide, step, 0)
    out_ref[...] = acc[:cols] + noise_ref[...] * pad[:cols]

    for half in range(2):
        for where in range(wide):
            to_sibling(where, half).wait_send()
        for line in range(lines):
            to_across(place(line, 0), half).wait_send()

            @pl.when((line <= z) & (z < lines - 1))
            def _():
                upward(place(line, 0), half).wait_send()

            @pl.when((line >= z) & (z > 0))
            def _():
                downward(place(line, 0), half).wait_send()


def solution(mesh):
    wide = mesh.shape["wide"]

    def body(points, probes, lengthscale, noise):
        feats, pts = points.shape
        cols = probes.shape[0]
        rows = feats + 32
        return pl.pallas_call(
            functools.partial(kernel, wide),
            out_shape=jax.ShapeDtypeStruct((cols, pts), jnp.float32),
            in_specs=[pl.BlockSpec(memory_space=pltpu.HBM)] * 4,
            out_specs=pl.BlockSpec(memory_space=pltpu.VMEM),
            scratch_shapes=[
                pltpu.VMEM((2 * wide, rows, pts), jnp.bfloat16),
                pltpu.VMEM((3 * feats + 32, pts), jnp.bfloat16),
                pltpu.VMEM((3 * feats + 32, pts), jnp.bfloat16),
                pltpu.VMEM((32, pts), jnp.float32),
                pltpu.VMEM((32, pts), jnp.float32),
                pltpu.VMEM((feats, pts), points.dtype),
                pltpu.VMEM((cols, pts), probes.dtype),
                pltpu.VMEM((1, feats), lengthscale.dtype),
                pltpu.VMEM((1, 1), noise.dtype),
                pltpu.SemaphoreType.DMA((4,)),
                pltpu.SemaphoreType.DMA((2 * wide,)),
                pltpu.SemaphoreType.DMA((2 * wide,)),
                pltpu.SemaphoreType.DMA((2 * wide,)),
                pltpu.SemaphoreType.DMA((2 * wide,)),
                pltpu.SemaphoreType.DMA((4 * wide,)),
            ],
            compiler_params=pltpu.CompilerParams(
                collective_id=0, has_side_effects=True, vmem_limit_bytes=64 * 2**20 - 2**17),
        )(points, probes, lengthscale[None], noise[None])

    placed = (
        P(None, ("trial", "wide", "narrow")),
        P(None, ("trial", "wide", "narrow")),
        P("trial"),
        P("trial"),
    )
    return jax.shard_map(
        body, mesh=mesh, in_specs=placed,
        out_specs=P(None, ("trial", "wide", "narrow")), check_vma=False)
```

```python
import functools
import math

import jax
import jax.numpy as jnp
from jax import lax
from jax.experimental import pallas as pl
from jax.experimental.pallas import tpu as pltpu
from jax.sharding import PartitionSpec as P

LOG2E = math.log2(math.e)
NT = (((1,), (1,)), ((), ()))
TN = (((0,), (0,)), ((), ()))


def three_parts(value):
    high = value.astype(jnp.bfloat16).astype(jnp.float32)
    rest = value - high
    middle = rest.astype(jnp.bfloat16).astype(jnp.float32)
    return high, middle, rest - middle


def kernel(wide, points_hbm, probes_hbm, length_hbm, noise_hbm, out_ref, held, own, visit, pad, acc,
           points_ref, probes_ref, length_ref, noise_ref, load_sem, sib_sem, side_sem, up_sem, down_sem,
           recv_sem):
    loads = [pltpu.make_async_copy(a, b, load_sem.at[i]) for i, (a, b) in enumerate(
        [(points_hbm, points_ref), (probes_hbm, probes_ref), (length_hbm, length_ref),
         (noise_hbm, noise_ref)])]
    for load in loads:
        load.start()
    t, w, c = lax.axis_index("trial"), lax.axis_index("wide"), lax.axis_index("narrow")
    feats, pts = points_ref.shape
    cols = probes_ref.shape[0]
    lines = wide // 2
    z, y = w // 2, w % 2
    upper = z * 2 // lines
    paired = z * (1 - upper) + (lines - 1 - z) * upper
    far = 4 * lines

    def at_rank(r):
        lone = (r + far - 2 * paired - 1) // far
        step = (1 - lone) * ((r + 1) // 2) * (2 * ((r + 1) % 2) - 1) + lone * (r - paired) * (1 - 2 * upper)
        return z + step

    def place(line, side):
        return line * 2 + y + side * (1 - 2 * y)

    across = place(z, 1)
    barrier = pltpu.get_barrier_semaphore()
    for peer in [(t, w, 1 - c), (t, across, c)]:
        pl.semaphore_signal(barrier, inc=1, device_id=peer, device_id_type=pl.DeviceIdType.MESH)

    @pl.when(z > 0)
    def _():
        pl.semaphore_signal(barrier, inc=1, device_id=(t, w - 2, c), device_id_type=pl.DeviceIdType.MESH)

    @pl.when(z < lines - 1)
    def _():
        pl.semaphore_signal(barrier, inc=1, device_id=(t, w + 2, c), device_id_type=pl.DeviceIdType.MESH)

    for load in loads:
        load.wait()
    mine = held.at[w * 2 + c]
    square = (feats, feats)
    diagonal = lax.broadcasted_iota(jnp.int32, square, 0) == lax.broadcasted_iota(jnp.int32, square, 1)
    length = jnp.sum(jnp.where(diagonal, length_ref[...], 0.0), axis=1, keepdims=True)
    scaled = (points_ref[...] / length).astype(jnp.bfloat16)
    wide_f = scaled.astype(jnp.float32)
    norm = jnp.sum(wide_f * wide_f, axis=0, keepdims=True)
    n_parts = three_parts((-0.5 * LOG2E) * norm)
    pad[...] = jnp.zeros_like(pad)
    pad[:cols] = probes_ref[...].astype(jnp.float32)
    row = lax.broadcasted_iota(jnp.int32, (32, pts), 0)
    tail = pad[...]
    mirror = jnp.zeros((32, pts), jnp.float32)
    for k, part in enumerate(n_parts):
        tail = jnp.where(row == cols + k, part, tail)
        tail = jnp.where(row == cols + 3 + k, 1.0, tail)
        mirror = jnp.where(row == cols + k, 1.0, mirror)
        mirror = jnp.where(row == cols + 3 + k, part, mirror)
    mine[:feats] = scaled
    mine[feats:] = tail.astype(jnp.bfloat16)

    ends = (z + lines - 1) // lines + (2 * lines - 2 - z) // lines
    pl.semaphore_wait(barrier, 2 + ends)

    def copy(where, half, sems, device):
        rows = pl.ds(half * feats, feats if half == 0 else 32)
        return pltpu.make_async_remote_copy(
            src_ref=held.at[where * 2 + c, rows], dst_ref=held.at[where * 2 + c, rows],
            send_sem=sems.at[where * 2 + half], recv_sem=recv_sem.at[(where * 2 + c) * 2 + half],
            device_id=device, device_id_type=pl.DeviceIdType.MESH)

    def arrived(slot, half):
        rows = pl.ds(half * feats, feats if half == 0 else 32)
        pltpu.make_async_remote_copy(
            src_ref=held.at[slot, rows], dst_ref=held.at[slot, rows],
            send_sem=sib_sem.at[half], recv_sem=recv_sem.at[slot * 2 + half],
            device_id=(t, w, 1 - c), device_id_type=pl.DeviceIdType.MESH).wait_recv()

    def to_sibling(where, half):
        return copy(where, half, sib_sem, (t, w, 1 - c))

    def to_across(where, half):
        return copy(where, half, side_sem, (t, across, c))

    def upward(where, half):
        return copy(where, half, up_sem, (t, w + 2, c))

    def downward(where, half):
        return copy(where, half, down_sem, (t, w - 2, c))

    for half in range(2):
        to_across(w, half).start()

        @pl.when(z < lines - 1)
        def _():
            upward(w, half).start()

        @pl.when(z > 0)
        def _():
            downward(w, half).start()

        to_sibling(w, half).start()

    for k, part in enumerate(three_parts(wide_f * LOG2E)):
        own[feats * k:feats * (k + 1)] = part.astype(jnp.bfloat16)
    own[3 * feats:] = mirror.astype(jnp.bfloat16)
    acc[...] = jnp.zeros_like(acc)

    def from_line(d, half):
        @pl.when(z - d >= 0)
        def _():
            below = w - 2 * d
            arrived(below * 2 + c, half)

            @pl.when(z < lines - 1)
            def _():
                upward(below, half).start()

            to_across(below, half).start()
            to_sibling(below, half).start()

        @pl.when(z + d < lines)
        def _():
            above = w + 2 * d
            arrived(above * 2 + c, half)

            @pl.when(z > 0)
            def _():
                downward(above, half).start()

            to_across(above, half).start()
            to_sibling(above, half).start()

    def where_of(k):
        odd, later, last = k % 2, (k + wide - 1) // wide, (k + 1) // wide
        rank = odd * ((k + 1) // 2 - last) + (1 - odd) * (k // 2 - later)
        return place(at_rank(rank), odd * last + (1 - odd) * later)

    def step(s, _):
        o, half = s // 2, s % 2
        slot = where_of(o) * 2 + c + half * (1 - 2 * c)

        @pl.when(s == 2)
        def _():
            from_line(1, 0)
            from_line(1, 1)

        @pl.when((s % 3 == 2) & (s >= 5))
        def _():
            from_line((s + 1) // 3, 0)

        @pl.when((s % 3 == 0) & (s >= 6))
        def _():
            from_line(s // 3, 1)

        @pl.when(half == 1)
        def _():
            arrived(slot, 0)
            arrived(slot, 1)
            k = o + 1

            @pl.when(((k % 2 == 0) & (k < wide)) | (k == wide - 1))
            def _():
                there = where_of(k)
                for part in range(2):
                    arrived(there * 2 + c, part)
                    to_sibling(there, part).start()

        block = held.at[slot]
        for k in range(3):
            visit[feats * k:feats * (k + 1)] = block[:feats]
        visit[3 * feats:] = block[feats:]
        cross = lax.dot_general(visit[...], own[...], TN, preferred_element_type=jnp.float32)
        tile = jnp.exp2(cross).astype(jnp.bfloat16)
        acc[...] += jnp.dot(block[feats:], tile, preferred_element_type=jnp.float32)
        return 0

    lax.fori_loop(0, 2 * wide, step, 0)
    out_ref[...] = acc[:cols] + noise_ref[...] * pad[:cols]

    for half in range(2):
        for where in range(wide):
            to_sibling(where, half).wait_send()
        for line in range(lines):
            to_across(place(line, 0), half).wait_send()

            @pl.when((line <= z) & (z < lines - 1))
            def _():
                upward(place(line, 0), half).wait_send()

            @pl.when((line >= z) & (z > 0))
            def _():
                downward(place(line, 0), half).wait_send()


def solution(mesh):
    wide = mesh.shape["wide"]

    def body(points, probes, lengthscale, noise):
        feats, pts = points.shape
        cols = probes.shape[0]
        rows = feats + 32
        return pl.pallas_call(
            functools.partial(kernel, wide),
            out_shape=jax.ShapeDtypeStruct((cols, pts), jnp.float32),
            in_specs=[pl.BlockSpec(memory_space=pltpu.HBM)] * 4,
            out_specs=pl.BlockSpec(memory_space=pltpu.VMEM),
            scratch_shapes=[
                pltpu.VMEM((2 * wide, rows, pts), jnp.bfloat16),
                pltpu.VMEM((3 * feats + 32, pts), jnp.bfloat16),
                pltpu.VMEM((3 * feats + 32, pts), jnp.bfloat16),
                pltpu.VMEM((32, pts), jnp.float32),
                pltpu.VMEM((32, pts), jnp.float32),
                pltpu.VMEM((feats, pts), points.dtype),
                pltpu.VMEM((cols, pts), probes.dtype),
                pltpu.VMEM((1, feats), lengthscale.dtype),
                pltpu.VMEM((1, 1), noise.dtype),
                pltpu.SemaphoreType.DMA((4,)),
                pltpu.SemaphoreType.DMA((2 * wide,)),
                pltpu.SemaphoreType.DMA((2 * wide,)),
                pltpu.SemaphoreType.DMA((2 * wide,)),
                pltpu.SemaphoreType.DMA((2 * wide,)),
                pltpu.SemaphoreType.DMA((4 * wide,)),
            ],
            compiler_params=pltpu.CompilerParams(
                collective_id=0, has_side_effects=True, vmem_limit_bytes=64 * 2**20 - 2**17),
        )(points, probes, lengthscale[None], noise[None])

    placed = (
        P(None, ("trial", "wide", "narrow")),
        P(None, ("trial", "wide", "narrow")),
        P("trial"),
        P("trial"),
    )
    return jax.shard_map(
        body, mesh=mesh, in_specs=placed,
        out_specs=P(None, ("trial", "wide", "narrow")), check_vma=False)
```
